32 devices in a mesh: col: 4 (over y, x), af: 8 (over z, core).
Axes of the slice: x: 2, y: 2, z: 4, core: 2. Of those that a mesh axis runs over, the one named last changes fastest.
Arguments:
- inputs: bfloat16 [2, 64, 64, 8, 256], P(None, 'col', 'af'), may hold values from -6 to 6
- first_filters: bfloat16 [3, 3, 3, 256, 256], P(None, None, None, 'af'), may hold values from -0.109375 to 0.109375
- second_filters: bfloat16 [3, 3, 3, 256, 256], P(None, None, None, 'af'), may hold values from -0.125 to 0.125
Outputs:
- features: bfloat16 [2, 32, 32, 4, 256], P(None, 'col', None, None, 'af')
The draws below stay inside these ranges and needn't reach their ends.
All inputs are finite; a program needn't handle non-finite values.
Results may differ from the reference program's by a relative error of at most 0.011.
Values may be sent and summed in bfloat16 or wider, within the bound.
A program may use at most 64 MiB of HBM per device.

```python
import jax
import jax.numpy as jnp
from jax import lax

C = 256
SAMPLES = 2
DEPTH = 64
HGT = 64
WID = 8


def raised(entries, key, source, target, shards_of, factor):
    def block_of(axis_at):
        return (jnp.arange(entries.shape[axis_at]) // (entries.shape[axis_at] // shards_of)).reshape((-1,) + (1,) * (entries.ndim - 1 - axis_at))

    first = jax.random.permutation(key, shards_of)[block_of(target)]
    second = (block_of(target) + shards_of // 2) % shards_of
    return jnp.where((block_of(source) == first) | (block_of(source) == second), factor * entries, entries)


def block_scale(stream_key, extent, cuts, smallest, largest):
    loudness = 1.0
    for axis_at, blocks in cuts:
        draws = jax.random.uniform(jax.random.fold_in(jax.random.fold_in(stream_key, 6), axis_at), (blocks,), jnp.float32, smallest / len(cuts), largest / len(cuts))
        loudness = loudness * jnp.repeat(jnp.exp(draws), extent[axis_at] // blocks).reshape((-1,) + (1,) * (len(extent) - 1 - axis_at))
    return loudness


def normal_values(own_key, extent, scale, limit, cuts=(), kind=jnp.bfloat16):
    factor_of = block_scale(own_key, extent, cuts, -0.22, 0.18) if cuts else 1.0
    values = jax.random.normal(own_key, extent, jnp.float32) * scale * factor_of
    return jnp.minimum(jnp.maximum(values, -limit), limit).astype(kind)


def heavy_noise(rng, shape, spread, most, split, heavy, dtype=jnp.bfloat16):
    drawn = spread * jax.random.normal(rng, shape, jnp.float32)
    if split:
        drawn = drawn * block_scale(rng, shape, split, -0.22, 0.18)
    return jnp.clip(raised(drawn, jax.random.fold_in(rng, 3), *heavy), -most, most).astype(dtype)


def setup_inputs(seed: int = 0) -> dict:
    arg_keys = jax.random.split(jax.random.key(seed), 4)
    return {
        "inputs": normal_values(arg_keys[0], (SAMPLES, DEPTH, HGT, WID, C), 1.0, 6.0, ((1, 4), (2, 8))),
        "first_filters": heavy_noise(arg_keys[1], (3, 3, 3, C, C), (27 * C) ** -0.5, 0.109375, ((3, 8),), (3, 4, 8, 2.0)),
        "second_filters": heavy_noise(arg_keys[2], (3, 3, 3, C, C), (27 * C // 2) ** -0.5, 0.125, ((3, 8),), (3, 4, 8, 2.0)),
    }


def convolve(volume, kernel, stride):
    return lax.conv_general_dilated(volume, kernel, (stride, stride, stride), ((1, 1), (1, 1), (1, 1)), dimension_numbers=("NDHWC", "DHWIO", "NDHWC"), preferred_element_type=jnp.float32)


def reference(inputs, first_filters, second_filters):
    hidden = jnp.maximum(convolve(inputs, first_filters, 1), 0.0).astype(jnp.bfloat16)
    return jnp.maximum(convolve(hidden, second_filters, 2), 0.0).astype(jnp.bfloat16)
```

```python
import jax
import jax.numpy as jnp
from jax import lax
from jax.sharding import PartitionSpec as P


def extended(block, axis, dim, low_width, high_width):
    count = lax.axis_size(axis)
    forward = [(i, i + 1) for i in range(count - 1)]
    backward = [(target, source) for source, target in forward]
    size = block.shape[dim]
    low = lax.ppermute(
        lax.slice_in_dim(block, size - low_width, None, axis=dim), axis, forward
    )
    high = lax.ppermute(lax.slice_in_dim(block, 0, high_width, axis=dim), axis, backward)
    return jnp.concatenate([low, block, high], axis=dim)


def convolve(volume, kernel, stride):
    return lax.conv_general_dilated(
        volume,
        kernel,
        (stride, stride, stride),
        ((0, 0), (0, 0), (1, 1)),
        dimension_numbers=("NDHWC", "DHWIO", "NDHWC"),
        preferred_element_type=jnp.float32,
    )


def per_device(inputs, first_filters, second_filters):
    first = lax.all_gather(first_filters, "af", axis=3, tiled=True)
    second = lax.all_gather(second_filters, "af", axis=3, tiled=True)
    block = extended(inputs, "col", 1, 2, 1)
    block = extended(block, "af", 2, 2, 1)
    hidden = jnp.maximum(convolve(block, first, 1), 0.0).astype(jnp.bfloat16)
    planes = lax.broadcasted_iota(jnp.int32, (1, hidden.shape[1], 1, 1, 1), 1)
    rows = lax.broadcasted_iota(jnp.int32, (1, 1, hidden.shape[2], 1, 1), 2)
    inside = (planes + lax.axis_index("col") > 0) & (rows + lax.axis_index("af") > 0)
    hidden = jnp.where(inside, hidden, jnp.zeros_like(hidden))
    features = jnp.maximum(convolve(hidden, second, 2), 0.0).astype(jnp.bfloat16)
    return lax.all_to_all(features, "af", split_axis=4, concat_axis=2, tiled=True)


def solution(mesh):
    placed = (
        P(None, "col", "af", None, None),
        P(None, None, None, "af", None),
        P(None, None, None, "af", None),
    )
    return jax.shard_map(
        per_device,
        mesh=mesh,
        in_specs=placed,
        out_specs=P(None, "col", None, None, "af"),
        check_vma=False,
    )
```

```python
import functools

import jax
import jax.numpy as jnp
from jax import lax
from jax.experimental import pallas as pl
from jax.experimental.pallas import tpu as pltpu
from jax.sharding import PartitionSpec as P

MESH = pl.DeviceIdType.MESH


def shifted_three(block, where_inside):
    w = lax.broadcasted_iota(jnp.int32, block.shape, 1)
    block = jnp.where(where_inside, block, 0.0)
    before = jnp.where(w == 0, 0.0, pltpu.roll(block, 1, 1))
    after = jnp.where(w == block.shape[1] - 1, 0.0, pltpu.roll(block, block.shape[1] - 1, 1))
    return before, block, after


def kernel(
    cols, rows_count,
    x_ref, first_ref, second_ref, out_ref,
    raw, taps_in, hidden, total, sums, packed, w_first, w_second,
    halo_send, halo_recv, local_sem,
    z_send, z_recv, xy_send, xy_recv, core_send, core_recv,
    out_send, out_recv,
):
    samples, depth, high, wid, chans = x_ref.shape
    shard = first_ref.shape[1]
    c = lax.axis_index("col")
    k = lax.axis_index("af")
    z, core = k // 2, lax.rem(k, 2)
    chips = rows_count // 2
    planes, lines = depth + 3, high + 3

    def at_col(e):
        return lax.rem(c + e + cols, cols)

    def at_row(e):
        return lax.rem(k + e + rows_count, rows_count)

    around = [(dc, dk) for dc in (-1, 0, 1) for dk in (-1, 0, 1) if (dc, dk) != (0, 0)]
    partners = [(c, at_row(e)) for e in range(1, rows_count)]
    partners += [(at_col(e), k) for e in range(1, cols)]
    partners += [(at_col(dc), at_row(dk)) for dc in (-1, 1) for dk in (-1, 1)]
    barrier = pltpu.get_barrier_semaphore()
    for partner in partners:
        pl.semaphore_signal(barrier, inc=1, device_id=partner, device_id_type=MESH)
    pl.semaphore_wait(barrier, len(partners))

    def remote(src, dst, send, recv, target):
        return pltpu.make_async_remote_copy(
            src_ref=src, dst_ref=dst, send_sem=send, recv_sem=recv,
            device_id=target, device_id_type=MESH,
        )

    def span(move, size):
        if move == 1:
            return pl.ds(size - 2, 2), pl.ds(0, 2)
        if move == -1:
            return pl.ds(0, 1), pl.ds(size + 2, 1)
        return pl.ds(0, size), pl.ds(2, size)

    pending = []
    other = (c, k + 1 - 2 * core)

    def rows_of(owner):
        return pl.ds(pl.multiple_of(owner * shard, shard), shard)

    half = shard // 2
    wide = chans // 2

    def quarter(gathered, owner, part):
        top = pl.multiple_of(owner * shard + (part // 2) * half, half)
        left = pl.multiple_of(lax.rem(part, 2) * wide, wide)
        return gathered.at[:, pl.ds(top, half), pl.ds(left, wide)]

    def own_quarter(source):
        top = pl.multiple_of((c // 2) * half, half)
        left = pl.multiple_of(lax.rem(c, 2) * wide, wide)
        return source.at[:, pl.ds(top, half), pl.ds(left, wide)]

    def begin_gather(n, source, gathered):
        for r in range(1, chips):
            target = (c, 2 * lax.rem(z + r, chips) + core)
            copy = remote(
                own_quarter(source), quarter(gathered, k, c),
                z_send.at[n, r - 1], z_recv.at[n, r - 1], target,
            )
            copy.start()
            pending.append(copy)
        mine = gathered.at[:, rows_of(k), :]
        copy = remote(source, mine, core_send.at[n, 0], core_recv.at[n, 0], other)
        copy.start()
        pending.append(copy)

    def owner_behind(r):
        return 2 * lax.rem(z - r + chips, chips) + core

    def pass_z(n, gathered):
        for r in range(1, chips):
            piece = quarter(gathered, owner_behind(r), c)
            remote(piece, piece, z_send.at[n, r - 1], z_recv.at[n, r - 1], other).wait_recv()
            for e in range(1, cols):
                copy = remote(
                    piece, piece, xy_send.at[n, r - 1, e - 1], xy_recv.at[n, r - 1, e - 1],
                    (at_col(e), k),
                )
                copy.start()
                pending.append(copy)
            copy = remote(piece, piece, core_send.at[n, r], core_recv.at[n, r], other)
            copy.start()
            pending.append(copy)

    def pass_xy(n, gathered):
        for r in range(1, chips):
            for e in range(1, cols):
                piece = quarter(gathered, owner_behind(r), at_col(-e))
                remote(
                    piece, piece, xy_send.at[n, r - 1, e - 1], xy_recv.at[n, r - 1, e - 1], other
                ).wait_recv()
                slot = chips + (r - 1) * (cols - 1) + e - 1
                copy = remote(piece, piece, core_send.at[n, slot], core_recv.at[n, slot], other)
                copy.start()
                pending.append(copy)

    def end_gather(n, gathered):
        mine = gathered.at[:, rows_of(k + 1 - 2 * core), :]
        remote(mine, mine, core_send.at[n, 0], core_recv.at[n, 0], other).wait_recv()
        for slot in range(1, chips + (chips - 1) * (cols - 1)):
            piece = quarter(gathered, k, c)
            remote(piece, piece, core_send.at[n, slot], core_recv.at[n, slot], other).wait_recv()

    begin_gather(0, first_ref, w_first)
    halos = []
    for i, (dc, dk) in enumerate(around):
        d_from, d_to = span(dc, depth)
        h_from, h_to = span(dk, high)
        copy = remote(
            x_ref.at[:, d_from, h_from], raw.at[:, d_to, h_to],
            halo_send.at[i], halo_recv.at[i], (at_col(dc), at_row(dk)),
        )
        copy.start()
        halos.append(copy)
    own = pltpu.make_async_copy(
        x_ref, raw.at[:, pl.ds(2, depth), pl.ds(2, high)], local_sem.at[0]
    )
    own.start()
    own_first = pltpu.make_async_copy(first_ref, w_first.at[:, rows_of(k), :], local_sem.at[1])
    own_second = pltpu.make_async_copy(second_ref, w_second.at[:, rows_of(k), :], local_sem.at[2])
    own_first.start()
    own_second.start()
    pass_z(0, w_first)
    begin_gather(1, second_ref, w_second)
    own.wait()
    for copy in halos:
        copy.wait()

    def prepare(d, carry):
        at_depth = c * depth + d - 2
        line = lax.broadcasted_iota(jnp.int32, (lines, wid, chans), 0) + k * high - 2
        inside = (
            (line >= 0) & (line < rows_count * high)
            & (at_depth >= 0) & (at_depth < cols * depth)
        )
        parts = [shifted_three(raw[s, d].astype(jnp.float32), inside) for s in range(samples)]
        for tap in range(3):
            both = jnp.concatenate([part[tap] for part in parts], axis=1)
            taps_in[d, :, :, tap * chans:(tap + 1) * chans] = both.astype(jnp.bfloat16)
        return carry

    lax.fori_loop(0, planes, prepare, 0)
    pass_xy(0, w_first)
    own_first.wait()
    end_gather(0, w_first)
    pass_z(1, w_second)

    deep, tall, cells = depth + 1, high + 1, samples * wid
    step = 3

    def first_tap(t, carry):
        a, b = t // 3, lax.rem(t, 3)
        weights = w_first[pl.ds(3 * t, 3)].reshape(3 * chans, chans)
        for j in range(tall // step):
            block = taps_in[pl.ds(a, deep), pl.ds(b + step * j, step)]
            product = jnp.dot(
                block.reshape(deep * step * cells, 3 * chans), weights,
                preferred_element_type=jnp.float32,
            ).reshape(deep, step, cells, chans)
            at = (slice(None), pl.ds(step * j, step))

            @pl.when(t == 0)
            def _():
                total[at] = product

            @pl.when(t > 0)
            def _():
                total[at] += product

        return carry

    lax.fori_loop(0, 9, first_tap, 0)
    pass_xy(1, w_second)

    def activate(d, carry):
        value = jnp.maximum(total[d], 0.0).reshape(tall * samples, wid, chans)
        line = lax.broadcasted_iota(jnp.int32, value.shape, 0) // samples
        inside = (line + k > 0) & (d + c > 0)
        for tap, part in enumerate(shifted_three(value, inside)):
            hidden[d, :, :, tap * chans:(tap + 1) * chans] = (
                part.reshape(tall, cells, chans).astype(jnp.bfloat16)
            )
        return carry

    lax.fori_loop(0, deep, activate, 0)
    own_second.wait()
    end_gather(1, w_second)

    d_out, h_out = depth // 2, high // 2
    sums[...] = jnp.zeros_like(sums)

    def second_tap(t, carry):
        a, b = t // 3, lax.rem(t, 3)
        weights = w_second[pl.ds(3 * t, 3)].reshape(3 * chans, chans)
        block = jnp.concatenate(
            [hidden[a + 2 * d, b + 2 * h] for d in range(d_out) for h in range(h_out)], axis=0
        )
        product = jnp.dot(block, weights, preferred_element_type=jnp.float32)
        for side in range(chans // 128):
            sums[side] += product[:, 128 * side:128 * (side + 1)]
        return carry

    lax.fori_loop(0, 9, second_tap, 0)

    count = d_out * h_out * cells // 2
    parts = 128 // (chans // rows_count)
    each = count // parts
    lane = lax.broadcasted_iota(jnp.int32, (each, 128), 1) // (chans // rows_count)
    for side in range(chans // 128):
        groups = [
            jnp.maximum(
                sums[side, pl.ds(2 * each * g, each, stride=2), :],
                0.0,
            )
            for g in range(parts)
        ]
        for q in range(parts):
            mixed = jnp.zeros((each, 128), jnp.float32)
            for g in range(parts):
                turn = ((g - q) % parts) * (chans // rows_count)
                value = pltpu.roll(groups[g], turn, 1) if turn else groups[g]
                mixed = jnp.where(lane == g, value, mixed)
            packed[side * parts + q] = mixed.astype(jnp.bfloat16)

    kept = pltpu.make_async_copy(packed.at[k], out_ref.at[k], local_sem.at[3])
    kept.start()
    sent = []
    for r in range(1, rows_count):
        copy = remote(
            packed.at[at_row(r)], out_ref.at[k],
            out_send.at[r - 1], out_recv.at[r - 1], (c, at_row(r)),
        )
        copy.start()
        sent.append(copy)
    for copy in pending:
        copy.wait_send()
    kept.wait()
    for copy in sent:
        copy.wait()


def fused(inputs, first_filters, second_filters):
    cols, rows_count = lax.axis_size("col"), lax.axis_size("af")
    samples, depth, high, wid, chans = inputs.shape
    shard = first_filters.shape[3]
    planes, lines, cells = depth + 3, high + 3, samples * wid
    d_out, h_out = depth // 2, high // 2
    count = d_out * h_out * cells // 2
    parts = 128 // (chans // rows_count)
    chips = rows_count // 2
    dma = pltpu.SemaphoreType.DMA
    slots = chips + (chips - 1) * (cols - 1)
    bf16, f32 = jnp.bfloat16, jnp.float32
    out = pl.pallas_call(
        functools.partial(kernel, cols, rows_count),
        out_shape=jax.ShapeDtypeStruct((rows_count, count // parts, 128), bf16),
        in_specs=[pl.BlockSpec(memory_space=pl.ANY)] * 3,
        out_specs=pl.BlockSpec(memory_space=pltpu.VMEM),
        scratch_shapes=[
            pltpu.VMEM((samples, planes, lines, wid, chans), bf16),
            pltpu.VMEM((planes, lines, cells, 3 * chans), bf16),
            pltpu.VMEM((depth + 1, high + 1, cells, 3 * chans), bf16),
            pltpu.VMEM((depth + 1, high + 1, cells, chans), f32),
            pltpu.VMEM((chans // 128, d_out * h_out * cells, 128), f32),
            pltpu.VMEM((rows_count, count // parts, 128), bf16),
            pltpu.VMEM((27, chans, chans), bf16),
            pltpu.VMEM((27, chans, chans), bf16),
            dma((8,)), dma((8,)), dma((4,)),
            dma((2, chips - 1)), dma((2, chips - 1)),
            dma((2, chips - 1, cols - 1)), dma((2, chips - 1, cols - 1)),
            dma((2, slots)), dma((2, slots)),
            dma((rows_count - 1,)), dma((rows_count - 1,)),
        ],
        compiler_params=pltpu.CompilerParams(
            collective_id=0, has_side_effects=True, vmem_limit_bytes=56 * 1024 * 1024
        ),
        cost_estimate=pl.CostEstimate(
            flops=12 * 10**9, bytes_accessed=16 * 10**6, transcendentals=0
        ),
    )(
        inputs,
        first_filters.reshape(27, shard, chans),
        second_filters.reshape(27, shard, chans),
    )
    low = d_out // parts
    out = out.reshape(rows_count, low, h_out, samples, wid // 2, parts, shard)
    out = out.transpose(3, 5, 1, 0, 2, 4, 6)
    return out.reshape(samples, d_out, rows_count * h_out, wid // 2, shard)


def extended(block, axis, dim, low_width, high_width):
    count = lax.axis_size(axis)
    forward = [(i, i + 1) for i in range(count - 1)]
    backward = [(target, source) for source, target in forward]
    size = block.shape[dim]
    low = lax.ppermute(
        lax.slice_in_dim(block, size - low_width, None, axis=dim), axis, forward
    )
    high = lax.ppermute(lax.slice_in_dim(block, 0, high_width, axis=dim), axis, backward)
    return jnp.concatenate([low, block, high], axis=dim)


def convolve(volume, kernel, stride):
    return lax.conv_general_dilated(
        volume,
        kernel,
        (stride, stride, stride),
        ((0, 0), (0, 0), (1, 1)),
        dimension_numbers=("NDHWC", "DHWIO", "NDHWC"),
        preferred_element_type=jnp.float32,
    )


def gathered_whole(inputs, first_filters, second_filters):
    first = lax.all_gather(first_filters, "af", axis=3, tiled=True)
    second = lax.all_gather(second_filters, "af", axis=3, tiled=True)
    block = extended(inputs, "col", 1, 2, 1)
    block = extended(block, "af", 2, 2, 1)
    hidden = jnp.maximum(convolve(block, first, 1), 0.0).astype(jnp.bfloat16)
    planes = lax.broadcasted_iota(jnp.int32, (1, hidden.shape[1], 1, 1, 1), 1)
    rows = lax.broadcasted_iota(jnp.int32, (1, 1, hidden.shape[2], 1, 1), 2)
    inside = (planes + lax.axis_index("col") > 0) & (rows + lax.axis_index("af") > 0)
    hidden = jnp.where(inside, hidden, jnp.zeros_like(hidden))
    features = jnp.maximum(convolve(hidden, second, 2), 0.0).astype(jnp.bfloat16)
    return lax.all_to_all(features, "af", split_axis=4, concat_axis=2, tiled=True)


def per_device(inputs, first_filters, second_filters):
    samples, depth, high, wid, chans = inputs.shape
    shard = first_filters.shape[3]
    fits = (
        lax.axis_size("col") == 4 and shard == 32 and chans == 256 and wid == 8
        and samples == 2 and depth % 8 == 0 and high % 6 == 2
    )
    plan = fused if fits else gathered_whole
    return plan(inputs, first_filters, second_filters)


def solution(mesh):
    placed = (
        P(None, "col", "af", None, None),
        P(None, None, None, "af", None),
        P(None, None, None, "af", None),
    )
    return jax.shard_map(
        per_device,
        mesh=mesh,
        in_specs=placed,
        out_specs=P(None, "col", None, None, "af"),
        check_vma=False,
    )
```

```python
import functools

import jax
import jax.numpy as jnp
from jax import lax
from jax.experimental import pallas as pl
from jax.experimental.pallas import tpu as pltpu
from jax.sharding import PartitionSpec as P

MESH = pl.DeviceIdType.MESH


def shifted_three(block, where_inside):
    w = lax.broadcasted_iota(jnp.int32, block.shape, 1)
    block = jnp.where(where_inside, block, 0.0)
    before = jnp.where(w == 0, 0.0, pltpu.roll(block, 1, 1))
    after = jnp.where(w == block.shape[1] - 1, 0.0, pltpu.roll(block, block.shape[1] - 1, 1))
    return before, block, after


def kernel(
    cols, rows_count,
    x_ref, first_ref, second_ref, out_ref,
    raw, taps_in, hidden, total, sums, packed, w_first, w_second,
    halo_send, halo_recv, local_sem,
    z_send, z_recv, xy_send, xy_recv, core_send, core_recv,
    out_send, out_recv,
):
    samples, depth, high, wid, chans = x_ref.shape
    shard = first_ref.shape[1]
    c = lax.axis_index("col")
    k = lax.axis_index("af")
    z, core = k // 2, lax.rem(k, 2)
    chips = rows_count // 2
    planes, lines = depth + 3, high + 3

    def at_col(e):
        return lax.rem(c + e + cols, cols)

    def at_row(e):
        return lax.rem(k + e + rows_count, rows_count)

    around = [(dc, dk) for dc in (-1, 0, 1) for dk in (-1, 0, 1) if (dc, dk) != (0, 0)]
    partners = [(c, at_row(e)) for e in range(1, rows_count)]
    partners += [(at_col(e), k) for e in range(1, cols)]
    partners += [(at_col(dc), at_row(dk)) for dc in (-1, 1) for dk in (-1, 1)]
    barrier = pltpu.get_barrier_semaphore()
    for partner in partners:
        pl.semaphore_signal(barrier, inc=1, device_id=partner, device_id_type=MESH)
    pl.semaphore_wait(barrier, len(partners))

    def remote(src, dst, send, recv, target):
        return pltpu.make_async_remote_copy(
            src_ref=src, dst_ref=dst, send_sem=send, recv_sem=recv,
            device_id=target, device_id_type=MESH,
        )

    def span(move, size):
        if move == 1:
            return pl.ds(size - 2, 2), pl.ds(0, 2)
        if move == -1:
            return pl.ds(0, 1), pl.ds(size + 2, 1)
        return pl.ds(0, size), pl.ds(2, size)

    pending = []
    other = (c, k + 1 - 2 * core)

    def rows_of(owner):
        return pl.ds(pl.multiple_of(owner * shard, shard), shard)

    half = shard // 2
    wide = chans // 2

    def quarter(gathered, owner, part):
        top = pl.multiple_of(owner * shard + (part // 2) * half, half)
        left = pl.multiple_of(lax.rem(part, 2) * wide, wide)
        return gathered.at[:, pl.ds(top, half), pl.ds(left, wide)]

    def own_quarter(source):
        top = pl.multiple_of((c // 2) * half, half)
        left = pl.multiple_of(lax.rem(c, 2) * wide, wide)
        return source.at[:, pl.ds(top, half), pl.ds(left, wide)]

    def begin_gather(n, source, gathered):
        for r in range(1, chips):
            target = (c, 2 * lax.rem(z + r, chips) + core)
            copy = remote(
                own_quarter(source), quarter(gathered, k, c),
                z_send.at[n, r - 1], z_recv.at[n, r - 1], target,
            )
            copy.start()
            pending.append(copy)
        mine = gathered.at[:, rows_of(k), :]
        copy = remote(source, mine, core_send.at[n, 0], core_recv.at[n, 0], other)
        copy.start()
        pending.append(copy)

    def owner_behind(r):
        return 2 * lax.rem(z - r + chips, chips) + core

    def pass_z(n, gathered):
        for r in range(1, chips):
            piece = quarter(gathered, owner_behind(r), c)
            remote(piece, piece, z_send.at[n, r - 1], z_recv.at[n, r - 1], other).wait_recv()
            for e in range(1, cols):
                copy = remote(
                    piece, piece, xy_send.at[n, r - 1, e - 1], xy_recv.at[n, r - 1, e - 1],
                    (at_col(e), k),
                )
                copy.start()
                pending.append(copy)
            copy = remote(piece, piece, core_send.at[n, r], core_recv.at[n, r], other)
            copy.start()
            pending.append(copy)

    def pass_xy(n, gathered):
        for r in range(1, chips):
            for e in range(1, cols):
                piece = quarter(gathered, owner_behind(r), at_col(-e))
                remote(
                    piece, piece, xy_send.at[n, r - 1, e - 1], xy_recv.at[n, r - 1, e - 1], other
                ).wait_recv()
                slot = chips + (r - 1) * (cols - 1) + e - 1
                copy = remote(piece, piece, core_send.at[n, slot], core_recv.at[n, slot], other)
                copy.start()
                pending.append(copy)

    def end_gather(n, gathered):
        mine = gathered.at[:, rows_of(k + 1 - 2 * core), :]
        remote(mine, mine, core_send.at[n, 0], core_recv.at[n, 0], other).wait_recv()
        for slot in range(1, chips + (chips - 1) * (cols - 1)):
            piece = quarter(gathered, k, c)
            remote(piece, piece, core_send.at[n, slot], core_recv.at[n, slot], other).wait_recv()

    gathers = [
        (first_ref.at[pl.ds(9 * a, 9)], w_first.at[pl.ds(9 * a, 9)]) for a in range(3)
    ]
    gathers.append((second_ref, w_second))
    halos = []
    for i, (dc, dk) in enumerate(around):
        d_from, d_to = span(dc, depth)
        h_from, h_to = span(dk, high)
        copy = remote(
            x_ref.at[:, d_from, h_from], raw.at[:, d_to, h_to],
            halo_send.at[i], halo_recv.at[i], (at_col(dc), at_row(dk)),
        )
        copy.start()
        halos.append(copy)
    own = pltpu.make_async_copy(
        x_ref, raw.at[:, pl.ds(2, depth), pl.ds(2, high)], local_sem.at[0]
    )
    own.start()
    own_first = pltpu.make_async_copy(first_ref, w_first.at[:, rows_of(k), :], local_sem.at[1])
    own_second = pltpu.make_async_copy(second_ref, w_second.at[:, rows_of(k), :], local_sem.at[2])
    own_first.start()
    own_second.start()
    for n in range(3):
        begin_gather(n, *gathers[n])
    pass_z(0, gathers[0][1])
    pass_z(1, gathers[1][1])
    pass_z(2, gathers[2][1])
    begin_gather(3, *gathers[3])
    own.wait()
    for copy in halos:
        copy.wait()

    def prepare(d, carry):
        at_depth = c * depth + d - 2
        line = lax.broadcasted_iota(jnp.int32, (lines, wid, chans), 0) + k * high - 2
        inside = (
            (line >= 0) & (line < rows_count * high)
            & (at_depth >= 0) & (at_depth < cols * depth)
        )
        parts = [shifted_three(raw[s, d].astype(jnp.float32), inside) for s in range(samples)]
        for tap in range(3):
            both = jnp.concatenate([part[tap] for part in parts], axis=1)
            taps_in[d, :, :, tap * chans:(tap + 1) * chans] = both.astype(jnp.bfloat16)
        return carry

    lax.fori_loop(0, planes, prepare, 0)
    own_first.wait()
    pass_xy(0, gathers[0][1])
    end_gather(0, gathers[0][1])

    deep, tall, cells = depth + 1, high + 1, samples * wid
    step = 3

    def first_layer(a):
        weights = w_first[pl.ds(9 * a, 9)].reshape(9 * chans, chans)
        for j in range(tall // step):
            block = jnp.concatenate(
                [
                    taps_in[pl.ds(a, deep), pl.ds(b + step * j, step)].reshape(
                        deep * step * cells, 3 * chans
                    )
                    for b in range(3)
                ],
                axis=1,
            )
            product = jnp.dot(block, weights, preferred_element_type=jnp.float32).reshape(
                deep, step, cells, chans
            )
            at = (slice(None), pl.ds(step * j, step))
            if a == 0:
                total[at] = product
            else:
                total[at] += product

    first_layer(0)
    pass_xy(1, gathers[1][1])
    end_gather(1, gathers[1][1])
    pass_z(3, w_second)
    first_layer(1)
    pass_xy(2, gathers[2][1])
    end_gather(2, gathers[2][1])
    first_layer(2)
    pass_xy(3, w_second)

    def activate(d, carry):
        value = jnp.maximum(total[d], 0.0).reshape(tall * samples, wid, chans)
        line = lax.broadcasted_iota(jnp.int32, value.shape, 0) // samples
        inside = (line + k > 0) & (d + c > 0)
        for tap, part in enumerate(shifted_three(value, inside)):
            hidden[d, :, :, tap * chans:(tap + 1) * chans] = (
                part.reshape(tall, cells, chans).astype(jnp.bfloat16)
            )
        return carry

    lax.fori_loop(0, deep, activate, 0)
    own_second.wait()
    end_gather(3, w_second)

    d_out, h_out = depth // 2, high // 2
    product = None
    for a in range(3):
        block = jnp.concatenate(
            [
                jnp.concatenate(
                    [hidden[a + 2 * d, b + 2 * h] for d in range(d_out) for h in range(h_out)],
                    axis=0,
                )
                for b in range(3)
            ],
            axis=1,
        )
        weights = w_second[pl.ds(9 * a, 9)].reshape(9 * chans, chans)
        term = jnp.dot(block, weights, preferred_element_type=jnp.float32)
        product = term if a == 0 else product + term
    for side in range(chans // 128):
        sums[side] = product[:, 128 * side:128 * (side + 1)]

    count = d_out * h_out * cells // 2
    parts = 128 // (chans // rows_count)
    each = count // parts
    lane = lax.broadcasted_iota(jnp.int32, (each, 128), 1) // (chans // rows_count)
    for side in range(chans // 128):
        groups = [
            jnp.maximum(
                sums[side, pl.ds(2 * each * g, each, stride=2), :],
                0.0,
            )
            for g in range(parts)
        ]
        for q in range(parts):
            mixed = jnp.zeros((each, 128), jnp.float32)
            for g in range(parts):
                turn = ((g - q) % parts) * (chans // rows_count)
                value = pltpu.roll(groups[g], turn, 1) if turn else groups[g]
                mixed = jnp.where(lane == g, value, mixed)
            packed[side * parts + q] = mixed.astype(jnp.bfloat16)

    kept = pltpu.make_async_copy(packed.at[k], out_ref.at[k], local_sem.at[3])
    kept.start()
    sent = []
    for r in range(1, rows_count):
        copy = remote(
            packed.at[at_row(r)], out_ref.at[k],
            out_send.at[r - 1], out_recv.at[r - 1], (c, at_row(r)),
        )
        copy.start()
        sent.append(copy)
    for copy in pending:
        copy.wait_send()
    kept.wait()
    for copy in sent:
        copy.wait()


def fused(inputs, first_filters, second_filters):
    cols, rows_count = lax.axis_size("col"), lax.axis_size("af")
    samples, depth, high, wid, chans = inputs.shape
    shard = first_filters.shape[3]
    planes, lines, cells = depth + 3, high + 3, samples * wid
    d_out, h_out = depth // 2, high // 2
    count = d_out * h_out * cells // 2
    parts = 128 // (chans // rows_count)
    chips = rows_count // 2
    dma = pltpu.SemaphoreType.DMA
    slots = chips + (chips - 1) * (cols - 1)
    bf16, f32 = jnp.bfloat16, jnp.float32
    out = pl.pallas_call(
        functools.partial(kernel, cols, rows_count),
        out_shape=jax.ShapeDtypeStruct((rows_count, count // parts, 128), bf16),
        in_specs=[pl.BlockSpec(memory_space=pl.ANY)] * 3,
        out_specs=pl.BlockSpec(memory_space=pltpu.VMEM),
        scratch_shapes=[
            pltpu.VMEM((samples, planes, lines, wid, chans), bf16),
            pltpu.VMEM((planes, lines, cells, 3 * chans), bf16),
            pltpu.VMEM((depth + 1, high + 1, cells, 3 * chans), bf16),
            pltpu.VMEM((depth + 1, high + 1, cells, chans), f32),
            pltpu.VMEM((chans // 128, d_out * h_out * cells, 128), f32),
            pltpu.VMEM((rows_count, count // parts, 128), bf16),
            pltpu.VMEM((27, chans, chans), bf16),
            pltpu.VMEM((27, chans, chans), bf16),
            dma((8,)), dma((8,)), dma((4,)),
            dma((4, chips - 1)), dma((4, chips - 1)),
            dma((4, chips - 1, cols - 1)), dma((4, chips - 1, cols - 1)),
            dma((4, slots)), dma((4, slots)),
            dma((rows_count - 1,)), dma((rows_count - 1,)),
        ],
        compiler_params=pltpu.CompilerParams(
            collective_id=0, has_side_effects=True, vmem_limit_bytes=56 * 1024 * 1024
        ),
        cost_estimate=pl.CostEstimate(
            flops=12 * 10**9, bytes_accessed=16 * 10**6, transcendentals=0
        ),
    )(
        inputs,
        first_filters.reshape(27, shard, chans),
        second_filters.reshape(27, shard, chans),
    )
    low = d_out // parts
    out = out.reshape(rows_count, low, h_out, samples, wid // 2, parts, shard)
    out = out.transpose(3, 5, 1, 0, 2, 4, 6)
    return out.reshape(samples, d_out, rows_count * h_out, wid // 2, shard)


def extended(block, axis, dim, low_width, high_width):
    count = lax.axis_size(axis)
    forward = [(i, i + 1) for i in range(count - 1)]
    backward = [(target, source) for source, target in forward]
    size = block.shape[dim]
    low = lax.ppermute(
        lax.slice_in_dim(block, size - low_width, None, axis=dim), axis, forward
    )
    high = lax.ppermute(lax.slice_in_dim(block, 0, high_width, axis=dim), axis, backward)
    return jnp.concatenate([low, block, high], axis=dim)


def convolve(volume, kernel, stride):
    return lax.conv_general_dilated(
        volume,
        kernel,
        (stride, stride, stride),
        ((0, 0), (0, 0), (1, 1)),
        dimension_numbers=("NDHWC", "DHWIO", "NDHWC"),
        preferred_element_type=jnp.float32,
    )


def gathered_whole(inputs, first_filters, second_filters):
    first = lax.all_gather(first_filters, "af", axis=3, tiled=True)
    second = lax.all_gather(second_filters, "af", axis=3, tiled=True)
    block = extended(inputs, "col", 1, 2, 1)
    block = extended(block, "af", 2, 2, 1)
    hidden = jnp.maximum(convolve(block, first, 1), 0.0).astype(jnp.bfloat16)
    planes = lax.broadcasted_iota(jnp.int32, (1, hidden.shape[1], 1, 1, 1), 1)
    rows = lax.broadcasted_iota(jnp.int32, (1, 1, hidden.shape[2], 1, 1), 2)
    inside = (planes + lax.axis_index("col") > 0) & (rows + lax.axis_index("af") > 0)
    hidden = jnp.where(inside, hidden, jnp.zeros_like(hidden))
    features = jnp.maximum(convolve(hidden, second, 2), 0.0).astype(jnp.bfloat16)
    return lax.all_to_all(features, "af", split_axis=4, concat_axis=2, tiled=True)


def per_device(inputs, first_filters, second_filters):
    samples, depth, high, wid, chans = inputs.shape
    shard = first_filters.shape[3]
    fits = (
        lax.axis_size("col") == 4 and shard == 32 and chans == 256 and wid == 8
        and samples == 2 and depth % 8 == 0 and high % 6 == 2
    )
    plan = fused if fits else gathered_whole
    return plan(inputs, first_filters, second_filters)


def solution(mesh):
    placed = (
        P(None, "col", "af", None, None),
        P(None, None, None, "af", None),
        P(None, None, None, "af", None),
    )
    return jax.shard_map(
        per_device,
        mesh=mesh,
        in_specs=placed,
        out_specs=P(None, "col", None, None, "af"),
        check_vma=False,
    )
```

```python
import functools

import jax
import jax.numpy as jnp
from jax import lax
from jax.experimental import pallas as pl
from jax.experimental.pallas import tpu as pltpu
from jax.sharding import PartitionSpec as P

MESH = pl.DeviceIdType.MESH


def shifted_three(block, where_inside):
    w = lax.broadcasted_iota(jnp.int32, block.shape, 1)
    block = jnp.where(where_inside, block, 0.0)
    before = jnp.where(w == 0, 0.0, pltpu.roll(block, 1, 1))
    after = jnp.where(w == block.shape[1] - 1, 0.0, pltpu.roll(block, block.shape[1] - 1, 1))
    return before, block, after


def kernel(
    cols, rows_count,
    x_ref, first_ref, second_ref, out_ref,
    raw, taps_in, hidden, total, sums, packed, w_first, w_second,
    halo_send, halo_recv, local_sem,
    z_send, z_recv, xy_send, xy_recv, core_send, core_recv,
    out_send, out_recv,
):
    samples, depth, high, wid, chans = x_ref.shape
    shard = first_ref.shape[1]
    c = lax.axis_index("col")
    k = lax.axis_index("af")
    z, core = k // 2, lax.rem(k, 2)
    chips = rows_count // 2
    planes, lines = depth + 3, high + 3

    def at_col(e):
        return lax.rem(c + e + cols, cols)

    def at_row(e):
        return lax.rem(k + e + rows_count, rows_count)

    around = [(dc, dk) for dc in (-1, 0, 1) for dk in (-1, 0, 1) if (dc, dk) != (0, 0)]
    partners = [(c, at_row(e)) for e in range(1, rows_count)]
    partners += [(at_col(e), k) for e in range(1, cols)]
    partners += [(at_col(dc), at_row(dk)) for dc in (-1, 1) for dk in (-1, 1)]
    barrier = pltpu.get_barrier_semaphore()
    for partner in partners:
        pl.semaphore_signal(barrier, inc=1, device_id=partner, device_id_type=MESH)
    pl.semaphore_wait(barrier, len(partners))

    def remote(src, dst, send, recv, target):
        return pltpu.make_async_remote_copy(
            src_ref=src, dst_ref=dst, send_sem=send, recv_sem=recv,
            device_id=target, device_id_type=MESH,
        )

    def span(move, size):
        if move == 1:
            return pl.ds(size - 2, 2), pl.ds(0, 2)
        if move == -1:
            return pl.ds(0, 1), pl.ds(size + 2, 1)
        return pl.ds(0, size), pl.ds(2, size)

    pending = []
    other = (c, k + 1 - 2 * core)

    def rows_of(owner):
        return pl.ds(pl.multiple_of(owner * shard, shard), shard)

    half = shard // 2
    wide = chans // 2

    def quarter(gathered, owner, part):
        top = pl.multiple_of(owner * shard + (part // 2) * half, half)
        left = pl.multiple_of(lax.rem(part, 2) * wide, wide)
        return gathered.at[:, pl.ds(top, half), pl.ds(left, wide)]

    def own_quarter(source):
        top = pl.multiple_of((c // 2) * half, half)
        left = pl.multiple_of(lax.rem(c, 2) * wide, wide)
        return source.at[:, pl.ds(top, half), pl.ds(left, wide)]

    def begin_gather(n, source, gathered):
        for r in range(1, chips):
            target = (c, 2 * lax.rem(z + r, chips) + core)
            copy = remote(
                own_quarter(source), quarter(gathered, k, c),
                z_send.at[n, r - 1], z_recv.at[n, r - 1], target,
            )
            copy.start()
            pending.append(copy)
        mine = gathered.at[:, rows_of(k), :]
        copy = remote(source, mine, core_send.at[n, 0], core_recv.at[n, 0], other)
        copy.start()
        pending.append(copy)

    def owner_behind(r):
        return 2 * lax.rem(z - r + chips, chips) + core

    def pass_z(n, gathered):
        for r in range(1, chips):
            piece = quarter(gathered, owner_behind(r), c)
            remote(piece, piece, z_send.at[n, r - 1], z_recv.at[n, r - 1], other).wait_recv()
            for e in range(1, cols):
                copy = remote(
                    piece, piece, xy_send.at[n, r - 1, e - 1], xy_recv.at[n, r - 1, e - 1],
                    (at_col(e), k),
                )
                copy.start()
                pending.append(copy)
            copy = remote(piece, piece, core_send.at[n, r], core_recv.at[n, r], other)
            copy.start()
            pending.append(copy)

    def pass_xy(n, gathered):
        for r in range(1, chips):
            for e in range(1, cols):
                piece = quarter(gathered, owner_behind(r), at_col(-e))
                remote(
                    piece, piece, xy_send.at[n, r - 1, e - 1], xy_recv.at[n, r - 1, e - 1], other
                ).wait_recv()
                slot = chips + (r - 1) * (cols - 1) + e - 1
                copy = remote(piece, piece, core_send.at[n, slot], core_recv.at[n, slot], other)
                copy.start()
                pending.append(copy)

    def end_gather(n, gathered):
        mine = gathered.at[:, rows_of(k + 1 - 2 * core), :]
        remote(mine, mine, core_send.at[n, 0], core_recv.at[n, 0], other).wait_recv()
        for slot in range(1, chips + (chips - 1) * (cols - 1)):
            piece = quarter(gathered, k, c)
            remote(piece, piece, core_send.at[n, slot], core_recv.at[n, slot], other).wait_recv()

    gathers = [
        (first_ref.at[pl.ds(9 * a, 9)], w_first.at[pl.ds(9 * a, 9)]) for a in range(3)
    ]
    gathers.append((second_ref, w_second))
    halos = []
    for i, (dc, dk) in enumerate(around):
        d_from, d_to = span(dc, depth)
        h_from, h_to = span(dk, high)
        copy = remote(
            x_ref.at[:, d_from, h_from], raw.at[:, d_to, h_to],
            halo_send.at[i], halo_recv.at[i], (at_col(dc), at_row(dk)),
        )
        copy.start()
        halos.append(copy)
    for n in range(3):
        begin_gather(n, *gathers[n])
    own = pltpu.make_async_copy(
        x_ref, raw.at[:, pl.ds(2, depth), pl.ds(2, high)], local_sem.at[0]
    )
    own.start()
    own_first = pltpu.make_async_copy(first_ref, w_first.at[:, rows_of(k), :], local_sem.at[1])
    own_second = pltpu.make_async_copy(second_ref, w_second.at[:, rows_of(k), :], local_sem.at[2])
    own_first.start()
    own_second.start()
    pass_z(0, gathers[0][1])
    own.wait()
    for copy in halos:
        copy.wait()

    def prepare(d, carry):
        at_depth = c * depth + d - 2
        line = lax.broadcasted_iota(jnp.int32, (lines, wid, chans), 0) + k * high - 2
        inside = (
            (line >= 0) & (line < rows_count * high)
            & (at_depth >= 0) & (at_depth < cols * depth)
        )
        parts = [shifted_three(raw[s, d].astype(jnp.float32), inside) for s in range(samples)]
        for tap in range(3):
            both = jnp.concatenate([part[tap] for part in parts], axis=1)
            taps_in[d, :, :, tap * chans:(tap + 1) * chans] = both.astype(jnp.bfloat16)
        return carry

    lax.fori_loop(0, planes // 2, prepare, 0)
    pass_z(1, gathers[1][1])
    lax.fori_loop(planes // 2, planes, prepare, 0)
    own_first.wait()
    pass_xy(0, gathers[0][1])
    pass_z(2, gathers[2][1])
    begin_gather(3, *gathers[3])
    end_gather(0, gathers[0][1])

    deep, tall, cells = depth + 1, high + 1, samples * wid
    step = 3

    def first_layer(a, following):
        weights = w_first[pl.ds(9 * a, 9)].reshape(9 * chans, chans)
        for j in range(tall // step):
            block = jnp.concatenate(
                [
                    taps_in[pl.ds(a, deep), pl.ds(b + step * j, step)].reshape(
                        deep * step * cells, 3 * chans
                    )
                    for b in range(3)
                ],
                axis=1,
            )
            product = jnp.dot(block, weights, preferred_element_type=jnp.float32).reshape(
                deep, step, cells, chans
            )
            at = (slice(None), pl.ds(step * j, step))
            if a == 0:
                total[at] = product
            else:
                total[at] += product
            if j == tall // step - 2:
                pass_xy(following, gathers[following][1])

    first_layer(0, 1)
    end_gather(1, gathers[1][1])
    pass_z(3, w_second)
    first_layer(1, 2)
    end_gather(2, gathers[2][1])
    first_layer(2, 3)

    def activate(d, carry):
        value = jnp.maximum(total[d], 0.0).reshape(tall * samples, wid, chans)
        line = lax.broadcasted_iota(jnp.int32, value.shape, 0) // samples
        inside = (line + k > 0) & (d + c > 0)
        for tap, part in enumerate(shifted_three(value, inside)):
            hidden[d, :, :, tap * chans:(tap + 1) * chans] = (
                part.reshape(tall, cells, chans).astype(jnp.bfloat16)
            )
        return carry

    lax.fori_loop(0, deep, activate, 0)
    own_second.wait()
    end_gather(3, w_second)

    d_out, h_out = depth // 2, high // 2
    product = None
    for a in range(3):
        block = jnp.concatenate(
            [
                jnp.concatenate(
                    [hidden[a + 2 * d, b + 2 * h] for d in range(d_out) for h in range(h_out)],
                    axis=0,
                )
                for b in range(3)
            ],
            axis=1,
        )
        weights = w_second[pl.ds(9 * a, 9)].reshape(9 * chans, chans)
        term = jnp.dot(block, weights, preferred_element_type=jnp.float32)
        product = term if a == 0 else product + term
    for side in range(chans // 128):
        sums[side] = product[:, 128 * side:128 * (side + 1)]

    count = d_out * h_out * cells // 2
    parts = 128 // (chans // rows_count)
    each = count // parts
    lane = lax.broadcasted_iota(jnp.int32, (each, 128), 1) // (chans // rows_count)
    for side in range(chans // 128):
        groups = [
            jnp.maximum(
                sums[side, pl.ds(2 * each * g, each, stride=2), :],
                0.0,
            )
            for g in range(parts)
        ]
        for q in range(parts):
            mixed = jnp.zeros((each, 128), jnp.float32)
            for g in range(parts):
                turn = ((g - q) % parts) * (chans // rows_count)
                value = pltpu.roll(groups[g], turn, 1) if turn else groups[g]
                mixed = jnp.where(lane == g, value, mixed)
            packed[side * parts + q] = mixed.astype(jnp.bfloat16)

    kept = pltpu.make_async_copy(packed.at[k], out_ref.at[k], local_sem.at[3])
    kept.start()
    sent = []
    for r in range(1, rows_count):
        copy = remote(
            packed.at[at_row(r)], out_ref.at[k],
            out_send.at[r - 1], out_recv.at[r - 1], (c, at_row(r)),
        )
        copy.start()
        sent.append(copy)
    for copy in pending:
        copy.wait_send()
    kept.wait()
    for copy in sent:
        copy.wait()


def fused(inputs, first_filters, second_filters):
    cols, rows_count = lax.axis_size("col"), lax.axis_size("af")
    samples, depth, high, wid, chans = inputs.shape
    shard = first_filters.shape[3]
    planes, lines, cells = depth + 3, high + 3, samples * wid
    d_out, h_out = depth // 2, high // 2
    count = d_out * h_out * cells // 2
    parts = 128 // (chans // rows_count)
    chips = rows_count // 2
    dma = pltpu.SemaphoreType.DMA
    slots = chips + (chips - 1) * (cols - 1)
    bf16, f32 = jnp.bfloat16, jnp.float32
    out = pl.pallas_call(
        functools.partial(kernel, cols, rows_count),
        out_shape=jax.ShapeDtypeStruct((rows_count, count // parts, 128), bf16),
        in_specs=[pl.BlockSpec(memory_space=pl.ANY)] * 3,
        out_specs=pl.BlockSpec(memory_space=pltpu.VMEM),
        scratch_shapes=[
            pltpu.VMEM((samples, planes, lines, wid, chans), bf16),
            pltpu.VMEM((planes, lines, cells, 3 * chans), bf16),
            pltpu.VMEM((depth + 1, high + 1, cells, 3 * chans), bf16),
            pltpu.VMEM((depth + 1, high + 1, cells, chans), f32),
            pltpu.VMEM((chans // 128, d_out * h_out * cells, 128), f32),
            pltpu.VMEM((rows_count, count // parts, 128), bf16),
            pltpu.VMEM((27, chans, chans), bf16),
            pltpu.VMEM((27, chans, chans), bf16),
            dma((8,)), dma((8,)), dma((4,)),
            dma((4, chips - 1)), dma((4, chips - 1)),
            dma((4, chips - 1, cols - 1)), dma((4, chips - 1, cols - 1)),
            dma((4, slots)), dma((4, slots)),
            dma((rows_count - 1,)), dma((rows_count - 1,)),
        ],
        compiler_params=pltpu.CompilerParams(
            collective_id=0, has_side_effects=True, vmem_limit_bytes=56 * 1024 * 1024
        ),
        cost_estimate=pl.CostEstimate(
            flops=12 * 10**9, bytes_accessed=16 * 10**6, transcendentals=0
        ),
    )(
        inputs,
        first_filters.reshape(27, shard, chans),
        second_filters.reshape(27, shard, chans),
    )
    low = d_out // parts
    out = out.reshape(rows_count, low, h_out, samples, wid // 2, parts, shard)
    out = out.transpose(3, 5, 1, 0, 2, 4, 6)
    return out.reshape(samples, d_out, rows_count * h_out, wid // 2, shard)


def extended(block, axis, dim, low_width, high_width):
    count = lax.axis_size(axis)
    forward = [(i, i + 1) for i in range(count - 1)]
    backward = [(target, source) for source, target in forward]
    size = block.shape[dim]
    low = lax.ppermute(
        lax.slice_in_dim(block, size - low_width, None, axis=dim), axis, forward
    )
    high = lax.ppermute(lax.slice_in_dim(block, 0, high_width, axis=dim), axis, backward)
    return jnp.concatenate([low, block, high], axis=dim)


def convolve(volume, kernel, stride):
    return lax.conv_general_dilated(
        volume,
        kernel,
        (stride, stride, stride),
        ((0, 0), (0, 0), (1, 1)),
        dimension_numbers=("NDHWC", "DHWIO", "NDHWC"),
        preferred_element_type=jnp.float32,
    )


def gathered_whole(inputs, first_filters, second_filters):
    first = lax.all_gather(first_filters, "af", axis=3, tiled=True)
    second = lax.all_gather(second_filters, "af", axis=3, tiled=True)
    block = extended(inputs, "col", 1, 2, 1)
    block = extended(block, "af", 2, 2, 1)
    hidden = jnp.maximum(convolve(block, first, 1), 0.0).astype(jnp.bfloat16)
    planes = lax.broadcasted_iota(jnp.int32, (1, hidden.shape[1], 1, 1, 1), 1)
    rows = lax.broadcasted_iota(jnp.int32, (1, 1, hidden.shape[2], 1, 1), 2)
    inside = (planes + lax.axis_index("col") > 0) & (rows + lax.axis_index("af") > 0)
    hidden = jnp.where(inside, hidden, jnp.zeros_like(hidden))
    features = jnp.maximum(convolve(hidden, second, 2), 0.0).astype(jnp.bfloat16)
    return lax.all_to_all(features, "af", split_axis=4, concat_axis=2, tiled=True)


def per_device(inputs, first_filters, second_filters):
    samples, depth, high, wid, chans = inputs.shape
    shard = first_filters.shape[3]
    fits = (
        lax.axis_size("col") == 4 and shard == 32 and chans == 256 and wid == 8 and high >= 8
        and samples == 2 and depth % 8 == 0 and high % 6 == 2
    )
    plan = fused if fits else gathered_whole
    return plan(inputs, first_filters, second_filters)


def solution(mesh):
    placed = (
        P(None, "col", "af", None, None),
        P(None, None, None, "af", None),
        P(None, None, None, "af", None),
    )
    return jax.shard_map(
        per_device,
        mesh=mesh,
        in_specs=placed,
        out_specs=P(None, "col", None, None, "af"),
        check_vma=False,
    )
```
